256 devices in a mesh: cmp: 32 (over y, z_hi, core), asy: 8 (over x, z_lo).
Axes of the slice: x: 4, y: 4, z: 8 (z_hi: 4, z_lo: 2; z = z_hi * 2 + z_lo), core: 2. Of those that a mesh axis runs over, the one named last changes fastest.
Arguments:
- comp_emb: bfloat16 [65536, 256], P(('cmp', 'asy')), may hold values from -6 to 6
- assay_emb: bfloat16 [32768, 256], P(('asy', 'cmp')), may hold values from -6 to 6
- bilinear: bfloat16 [256, 256], replicated, may hold values from -3 to 3
- tile_pos: int32 [128, 64], P('cmp', 'asy'), may hold values 0 or 1
Outputs:
- grad_comp: float32 [65536, 256], P(('cmp', 'asy'))
- grad_assay: float32 [32768, 256], P(('asy', 'cmp'))
- grad_bilinear: float32 [256, 256], replicated
The draws below stay inside these ranges and needn't reach their ends.
All inputs are finite; a program needn't handle non-finite values. No bound on the sum of `tile_pos` on one device may be relied on, other than what follows from the above.
Results may differ from the reference program's by a relative error of at most 0.0004.
The reference program's roundings to bfloat16 on the way (of `query` and `slope`) count: a program that leaves them out, or rounds other values in their place, can miss the bound.
Values may be sent and summed in bfloat16 or wider, within the bound.
A program may use at most 128 MiB of HBM per device.

```python
import math
import jax
import jax.numpy as jnp
from jax import lax

D = 256
TILE = 512
NC = 65536
NA = 32768


def place_ends(values, stream_key, low, largest):
    spot = [jax.random.randint(jax.random.fold_in(stream_key, axis), (), 0, length) for axis, length in enumerate(values.shape)]
    main_axis = values.shape.index(max(values.shape))
    next_to = spot[:main_axis] + [(spot[main_axis] + 1) % values.shape[main_axis]] + spot[main_axis + 1:]
    return values.at[tuple(spot)].set(low).at[tuple(next_to)].set(largest)


def shard_levels(rng, shape, split, least, largest):
    level = 1.0
    for axis_at, parts in split:
        heights = jax.random.uniform(jax.random.fold_in(jax.random.fold_in(rng, 6), axis_at), (parts,), jnp.float32, least / len(split), largest / len(split))
        level = level * jnp.repeat(jnp.exp(heights), shape[axis_at] // parts).reshape((-1,) + (1,) * (len(shape) - 1 - axis_at))
    return level


def normal_values(key, extent, width, limit, shards=(), kind=jnp.bfloat16):
    drawn = jax.random.normal(key, extent, jnp.float32) * width
    if len(shards) > 0:
        drawn = shard_levels(key, extent, shards, -0.22, 0.18) * drawn
    return jnp.clip(drawn, min=-limit, max=limit).astype(kind)


def setup_inputs(seed: int = 0) -> dict:
    key_of = jax.random.split(jax.random.key(seed), 5)
    comp_emb = normal_values(key_of[0], (NC, D), 1.0, 6.0, ((0, 256),))
    assay_emb = normal_values(key_of[1], (NA, D), 1.0, 6.0, ((0, 256),))
    bilinear = normal_values(key_of[2], (D, D), (3.0 / D ** 0.5), 3.0)
    tile_pos = place_ends((jax.random.randint(key_of[3], (NC // TILE, NA // TILE), 0, 4) < 1).astype(jnp.int32), jax.random.fold_in(key_of[3], 1), 0, 1)
    return {"comp_emb": comp_emb, "assay_emb": assay_emb, "bilinear": bilinear, "tile_pos": tile_pos}


def reference(comp_emb, assay_emb, bilinear, tile_pos):
    blocks = comp_emb.reshape(NC // TILE, TILE, D)
    scale = 1.0 / math.sqrt(D)

    def step(carry, item):
        block, tile_row = item
        query = jnp.dot(block, bilinear, preferred_element_type=jnp.float32).astype(jnp.bfloat16)
        scores = jnp.dot(query, assay_emb.T, preferred_element_type=jnp.float32) * scale
        labels = jnp.repeat(tile_row, TILE).astype(jnp.float32)
        slope = (jax.nn.sigmoid(scores) - labels[None, :]).astype(jnp.bfloat16)
        pulled = jnp.dot(slope, assay_emb, preferred_element_type=jnp.float32)
        carry = carry + jnp.dot(slope.T, query, preferred_element_type=jnp.float32)
        return (carry, pulled)
    start = jnp.zeros((NA, D), jnp.float32)
    assay_terms, pulled = lax.scan(step, start, (blocks, tile_pos))
    pulled = pulled.reshape(NC, D)
    grad_comp = jnp.dot(pulled, bilinear.astype(jnp.float32).T, precision=lax.Precision.HIGHEST) / math.sqrt(NA)
    grad_assay = assay_terms / math.sqrt(NC)
    grad_bilinear = jnp.dot(comp_emb.astype(jnp.float32).T, pulled, precision=lax.Precision.HIGHEST) / math.sqrt(NC * NA)
    return (grad_comp, grad_assay, grad_bilinear)
```

```python
import functools
import math

import jax
import jax.numpy as jnp
from jax import lax
from jax.experimental import pallas as pl
from jax.experimental.pallas import tpu as pltpu
from jax.sharding import PartitionSpec as P

MESH = pl.DeviceIdType.MESH
NN = (((1,), (0,)), ((), ()))
NT = (((1,), (1,)), ((), ()))
TN = (((0,), (0,)), ((), ()))
LEVELS = 32000.0
CODE_ROWS = 16
RING = 4


def dot(lhs, rhs, dims):
    return lax.dot_general(lhs, rhs, dims, preferred_element_type=jnp.float32)


def split_bf16(value):
    high = value.astype(jnp.bfloat16)
    low = (value - high.astype(jnp.float32)).astype(jnp.bfloat16)
    return high, low


def encode(value, target, row):
    rows = value.shape[0]
    top = jnp.maximum(jnp.max(jnp.abs(value), axis=0, keepdims=True), 1e-30)
    code = jnp.ceil(jnp.log2(top) * 256.0) + 1.0
    scale = LEVELS * jnp.exp2(code * (-1.0 / 256.0))
    target[pl.ds(row, rows), :] = jnp.round(value * scale).astype(jnp.int32).astype(jnp.int16)
    target[pl.ds(row + rows, CODE_ROWS), :] = (
        jnp.broadcast_to(code, (CODE_ROWS, value.shape[1])).astype(jnp.int32).astype(jnp.int16)
    )


def decode(source, row, rows):
    code = source[pl.ds(row + rows, CODE_ROWS), :].astype(jnp.int32).astype(jnp.float32)[0:1, :]
    unit = jnp.exp2(code * (1.0 / 256.0)) * (1.0 / LEVELS)
    return source[pl.ds(row, rows), :].astype(jnp.int32).astype(jnp.float32) * unit


class Sends:
    def __init__(self, send_sems, recv_sems):
        self.send_sems, self.recv_sems = send_sems, recv_sems
        self.count = 0
        self.started = []

    def make(self, source, target, device):
        index = self.count
        self.count += 1
        return pltpu.make_async_remote_copy(
            src_ref=source,
            dst_ref=target,
            send_sem=self.send_sems.at[index],
            recv_sem=self.recv_sems.at[index],
            device_id=device,
            device_id_type=MESH,
        )

    def start(self, source, target, device):
        copy = self.make(source, target, device)
        copy.start()
        self.started.append(copy)
        return copy

    def finish(self):
        for copy in self.started:
            copy.wait_send()


SENDS = 80


def kernel(
    totals,
    tile_pos,
    comp_ref,
    assay_ref,
    bil_ref,
    gc_ref,
    ga_ref,
    gb_ref,
    comps,
    assays,
    query,
    slope,
    pulled,
    grads,
    grads_in,
    pull_out,
    pull_in,
    pull_z_out,
    pull_z_in,
    grad_out,
    grad_in,
    grad_z_out,
    grad_z_in,
    weight,
    weight_x,
    weight_y,
    weight_z,
    weight_l,
    weight_c,
    weight_g,
    send_sems,
    recv_sems,
    local_sems,
):
    total_comp, total_assay, width = totals
    cmp, asy = lax.axis_index("cmp"), lax.axis_index("asy")
    c, zh, y = cmp % 2, (cmp // 2) % RING, cmp // (2 * RING)
    zl, x = asy % 2, asy // 2
    oc = 1 - c

    def at(y_=None, zh_=None, c_=None, x_=None, zl_=None):
        y_ = y if y_ is None else y_
        zh_ = zh if zh_ is None else zh_
        c_ = c if c_ is None else c_
        x_ = x if x_ is None else x_
        zl_ = zl if zl_ is None else zl_
        return ((y_ * RING + zh_) * 2 + c_, x_ * 2 + zl_)

    def turn(place, step):
        return lax.rem(place + step, RING)

    AWAY = (1, 3, 2)
    peer_c = at(c_=oc)
    peer_l = at(zl_=1 - zl)
    peer_x = {d: at(x_=turn(x, d)) for d in AWAY}
    peer_y = {d: at(y_=turn(y, d)) for d in AWAY}
    peer_z = {d: at(zh_=turn(zh, d)) for d in AWAY}
    partners = [peer_c, peer_l, *peer_x.values(), *peer_y.values(), *peer_z.values()]

    barrier = pltpu.get_barrier_semaphore()
    for partner in partners:
        pl.semaphore_signal(barrier, inc=1, device_id=partner, device_id_type=MESH)

    rows_c, rows_a = comp_ref.shape[0], assay_ref.shape[0]
    own_comp = pltpu.make_async_copy(comp_ref, comps.at[x, pl.ds(zl * rows_c, rows_c)], local_sems.at[0])
    own_assay = pltpu.make_async_copy(assay_ref, assays.at[c, y, pl.ds(zh * rows_a, rows_a)], local_sems.at[1])
    own_comp.start()
    own_assay.start()
    pl.semaphore_wait(barrier, len(partners))

    net = Sends(send_sems, recv_sems)

    def comp_rows(x_, zl_):
        return comps.at[x_, pl.ds(zl_ * rows_c, rows_c)]

    def assay_rows(y_, zh_):
        return assays.at[c, y_, pl.ds(zh_ * rows_a, rows_a)]

    c_l = net.start(comp_ref, comp_rows(x, zl), peer_l)
    a_z = {d: net.start(assay_ref, assay_rows(y, zh), peer_z[d]) for d in AWAY}
    c_x, c_f, a_y, a_f = {}, {}, {}, {}
    for d in AWAY:
        c_x[d] = net.start(comp_ref, comp_rows(x, zl), peer_x[d])
        a_y[d] = net.start(assay_ref, assay_rows(y, zh), peer_y[d])

    def make_query(k, row, rows):
        block = comps[k, pl.ds(row, rows), :]
        query[k, pl.ds(row, rows), :] = dot(block, bil_ref[...], NN).astype(jnp.bfloat16)

    pulled[...] = jnp.zeros_like(pulled)
    own_comp.wait()
    make_query(x, zl * rows_c, rows_c)
    c_l.wait_recv()
    for d in AWAY:
        block = comp_rows(x, 1 - zl)
        c_f[d] = net.start(block, block, peer_x[d])
    make_query(x, (1 - zl) * rows_c, rows_c)
    own_assay.wait()
    for d in AWAY:
        a_z[d].wait_recv()
        block = assay_rows(y, turn(zh, RING - d))
        for e in AWAY:
            a_f[d, e] = net.start(block, block, peer_y[e])

    a_c = {}

    def share(d):
        block = assays.at[c, turn(y, RING - d)]
        a_c[d] = net.start(block, block, peer_c)

    share(0)

    scale = 1.0 / math.sqrt(width)
    half = slope.shape[3] // 2

    def score(k, cc, l):
        chunk = assays[cc, l]
        q = query[k]
        scores = dot(q * jnp.bfloat16(scale), chunk, NT)
        sig = 1.0 / (1.0 + jnp.exp(-scores))
        for h in range(2):
            label = tile_pos[k, 2 * l + h].astype(jnp.float32)
            slope[k, cc * RING + l, :, h * half : (h + 1) * half] = (
                sig[:, h * half : (h + 1) * half] - label
            ).astype(jnp.bfloat16)
        pulled[k] = pulled[k] + dot(slope[k, cc * RING + l], chunk, NN)

    def score_near(cc, l):
        @pl.loop(0, 3)
        def _(i):
            score(turn(x, i + i // 2), cc, l)

    def arrive_assay(d):
        a_y[d].wait_recv()
        for e in AWAY:
            a_f[e, d].wait_recv()
        share(d)

    def arrive_comp(d):
        c_x[d].wait_recv()
        c_f[d].wait_recv()
        make_query(turn(x, RING - d), 0, 2 * rows_c)

    l1, l3, l2 = turn(y, 3), turn(y, 1), turn(y, 2)
    score(x, c, y)
    a_c[0].wait_recv()
    score(x, oc, y)
    arrive_comp(1)
    arrive_comp(3)
    arrive_assay(1)
    arrive_assay(3)

    @pl.loop(0, 2)
    def _(i):
        k = turn(x, 1 + 2 * i)
        score(k, c, y)
        score(k, oc, y)

    score_near(c, l1)
    score_near(c, l3)
    a_c[1].wait_recv()
    score_near(oc, l1)
    a_c[3].wait_recv()
    score_near(oc, l3)
    arrive_assay(2)
    arrive_comp(2)
    score_near(c, l2)
    a_c[2].wait_recv()
    score_near(oc, l2)

    def send_pulled(d):
        k = turn(x, d)
        slot = AWAY.index(d)
        for h in range(2):
            encode(pulled[k, h * rows_c : (h + 1) * rows_c, :], pull_out.at[slot], h * (rows_c + CODE_ROWS))
        return net.start(pull_out.at[slot], pull_in.at[slot], peer_x[d])

    p_x = {1: send_pulled(1), 3: send_pulled(3)}

    k2 = turn(x, 2)
    score(k2, c, l2)
    score(k2, oc, l2)

    def grad(cc, l):
        left = slope[:, cc * RING + l].reshape(RING * slope.shape[2], slope.shape[3])
        right = query[...].reshape(RING * query.shape[1], query.shape[2])
        grads[cc, l] = dot(left, right, TN)

    g_c, g_y = {}, {}

    def grad_both(d):
        l = turn(y, d)
        grad(oc, l)
        g_c[d] = net.start(grads.at[oc, l], grads_in.at[l], peer_c)
        grad(c, l)

    def send_grad(d):
        l = turn(y, d)
        g_c[d].wait_recv()
        slot = AWAY.index(d)
        for h in range(RING):
            rows = pl.ds(h * rows_a, rows_a)
            encode(grads[c, l, rows, :] + grads_in[l, rows, :], grad_out.at[slot], h * (rows_a + CODE_ROWS))
        g_y[d] = net.start(grad_out.at[slot], grad_in.at[slot], peer_y[d])

    grad_both(2)

    @pl.loop(0, 4)
    def _(i):
        l = turn(y, 1 + 2 * (i % 2))
        score(k2, (c + i // 2) % 2, l)

    score(k2, c, y)
    score(k2, oc, y)
    p_x[2] = send_pulled(2)
    send_grad(2)
    grad_both(1)
    grad_both(3)
    send_grad(1)

    def weight_term(k):
        high, low = split_bf16(pulled[k])
        return dot(comps[k], high, TN) + dot(comps[k], low, TN)

    weight[...] = jnp.zeros_like(weight)

    @pl.loop(0, RING)
    def _(k):
        weight[...] += weight_term(k)

    part_x, part_y = width // RING, width // RING // RING
    w_x = {}
    for d in AWAY:
        w_x[d] = net.start(
            weight.at[pl.ds(turn(x, d) * part_x, part_x)], weight_x.at[AWAY.index(d)], peer_x[d]
        )
    send_grad(3)
    grad_both(0)

    w_y = {}
    for d in AWAY:
        w_x[d].wait_recv()
    mine = weight.at[pl.ds(x * part_x, part_x)]
    mine[...] = mine[...] + weight_x[0] + weight_x[1] + weight_x[2]
    for d in AWAY:
        w_y[d] = net.start(
            weight.at[pl.ds(x * part_x + turn(y, d) * part_y, part_y)],
            weight_y.at[AWAY.index(d)],
            peer_y[d],
        )

    for d in AWAY:
        p_x[d].wait_recv()

    def pulled_rows(h):
        value = pulled[x, pl.ds(h * rows_c, rows_c), :]
        for slot in range(3):
            value = value + decode(pull_in.at[slot], h * (rows_c + CODE_ROWS), rows_c)
        return value

    encode(pulled_rows(1 - zl), pull_z_out, 0)
    p_l = net.start(pull_z_out, pull_z_in, peer_l)

    w_z = {}
    for d in AWAY:
        w_y[d].wait_recv()
    mine_y = weight[pl.ds(x * part_x + y * part_y, part_y), :]
    weight_z[zh] = mine_y + weight_y[0] + weight_y[1] + weight_y[2]
    for d in AWAY:
        w_z[d] = net.start(weight_z.at[zh], weight_z.at[zh], peer_z[d])

    pulled_own = pulled_rows(zl)
    p_l.wait_recv()
    high, low = split_bf16(pulled_own + decode(pull_z_in, 0, rows_c))
    gc_ref[...] = (dot(high, bil_ref[...], NT) + dot(low, bil_ref[...], NT)) * (1.0 / math.sqrt(total_assay))

    g_c[0].wait_recv()
    for d in AWAY:
        g_y[d].wait_recv()

    def grad_rows(h):
        rows = pl.ds(h * rows_a, rows_a)
        value = grads[c, y, rows, :] + grads_in[y, rows, :]
        for slot in range(3):
            value = value + decode(grad_in.at[slot], h * (rows_a + CODE_ROWS), rows_a)
        return value

    g_z = {}
    for d in (2, 1, 3):
        slot = AWAY.index(d)
        encode(grad_rows(turn(zh, d)), grad_z_out.at[slot], 0)
        g_z[d] = net.start(grad_z_out.at[slot], grad_z_in.at[slot], peer_z[d])

    for d in AWAY:
        w_z[d].wait_recv()
    weight_l[0] = (weight_z[0] + weight_z[1]) + (weight_z[2] + weight_z[3])
    w_l = net.start(weight_l.at[0], weight_l.at[1], peer_l)
    grad_own = grad_rows(zh)
    w_l.wait_recv()
    weight_c[0] = weight_l[0] + weight_l[1]
    w_c = net.start(weight_c.at[0], weight_c.at[1], peer_c)
    w_c.wait_recv()
    weight_g[pl.ds(y * part_y, part_y), :] = (weight_c[0] + weight_c[1]) * (
        1.0 / math.sqrt(total_comp * total_assay)
    )
    block = weight_g.at[pl.ds(y * part_y, part_y)]
    w_gy = [net.start(block, block, peer_y[d]) for d in AWAY]
    for copy in w_gy:
        copy.wait_recv()
    gb_ref[pl.ds(x * part_x, part_x), :] = weight_g[...]
    block = gb_ref.at[pl.ds(x * part_x, part_x)]
    w_gx = [net.start(weight_g, block, peer_x[d]) for d in AWAY]

    for d in AWAY:
        g_z[d].wait_recv()
    for slot in range(3):
        grad_own = grad_own + decode(grad_z_in.at[slot], 0, rows_a)
    ga_ref[...] = grad_own * (1.0 / math.sqrt(total_comp))
    for copy in w_gx:
        copy.wait_recv()
    net.finish()


def local(comp_emb, assay_emb, bilinear, tile_pos):
    size_cmp, size_asy = lax.axis_size("cmp"), lax.axis_size("asy")
    rows_c, width = comp_emb.shape
    rows_a = assay_emb.shape[0]
    total_comp, total_assay = rows_c * size_cmp * size_asy, rows_a * size_cmp * size_asy
    group_c, group_a = rows_c * 2, rows_a * RING
    part = width // RING
    vmem = pl.BlockSpec(memory_space=pltpu.VMEM)
    block_c, block_a = rows_c + CODE_ROWS, rows_a + CODE_ROWS
    return tuple(
        pl.pallas_call(
            functools.partial(kernel, (total_comp, total_assay, width)),
            out_shape=[
                jax.ShapeDtypeStruct((rows_c, width), jnp.float32),
                jax.ShapeDtypeStruct((rows_a, width), jnp.float32),
                jax.ShapeDtypeStruct((width, width), jnp.float32),
            ],
            in_specs=[
                pl.BlockSpec(memory_space=pltpu.SMEM),
                pl.BlockSpec(memory_space=pl.ANY),
                pl.BlockSpec(memory_space=pl.ANY),
                vmem,
            ],
            out_specs=[vmem, vmem, vmem],
            scratch_shapes=[
                pltpu.VMEM((RING, group_c, width), jnp.bfloat16),
                pltpu.VMEM((2, RING, group_a, width), jnp.bfloat16),
                pltpu.VMEM((RING, group_c, width), jnp.bfloat16),
                pltpu.VMEM((RING, 2 * RING, group_c, group_a), jnp.bfloat16),
                pltpu.VMEM((RING, group_c, width), jnp.float32),
                pltpu.VMEM((2, RING, group_a, width), jnp.float32),
                pltpu.VMEM((RING, group_a, width), jnp.float32),
                pltpu.VMEM((3, 2 * block_c, width), jnp.int16),
                pltpu.VMEM((3, 2 * block_c, width), jnp.int16),
                pltpu.VMEM((block_c, width), jnp.int16),
                pltpu.VMEM((block_c, width), jnp.int16),
                pltpu.VMEM((3, RING * block_a, width), jnp.int16),
                pltpu.VMEM((3, RING * block_a, width), jnp.int16),
                pltpu.VMEM((3, block_a, width), jnp.int16),
                pltpu.VMEM((3, block_a, width), jnp.int16),
                pltpu.VMEM((width, width), jnp.float32),
                pltpu.VMEM((3, part, width), jnp.float32),
                pltpu.VMEM((3, part // RING, width), jnp.float32),
                pltpu.VMEM((RING, part // RING, width), jnp.float32),
                pltpu.VMEM((2, part // RING, width), jnp.float32),
                pltpu.VMEM((2, part // RING, width), jnp.float32),
                pltpu.VMEM((part, width), jnp.float32),
                pltpu.SemaphoreType.DMA((SENDS,)),
                pltpu.SemaphoreType.DMA((SENDS,)),
                pltpu.SemaphoreType.DMA((2,)),
            ],
            compiler_params=pltpu.CompilerParams(
                collective_id=0, has_side_effects=True, vmem_limit_bytes=58 * 2**20
            ),
            name="link_grads",
        )(tile_pos, comp_emb, assay_emb, bilinear)
    )


def solution(mesh):
    return jax.shard_map(
        local,
        mesh=mesh,
        in_specs=(P(("cmp", "asy"), None), P(("asy", "cmp"), None), P(), P("cmp", "asy")),
        out_specs=(P(("cmp", "asy"), None), P(("asy", "cmp"), None), P()),
        check_vma=False,
    )
```

```python
import functools
import math

import jax
import jax.numpy as jnp
from jax import lax
from jax.experimental import pallas as pl
from jax.experimental.pallas import tpu as pltpu
from jax.sharding import PartitionSpec as P

MESH = pl.DeviceIdType.MESH
NN = (((1,), (0,)), ((), ()))
NT = (((1,), (1,)), ((), ()))
TN = (((0,), (0,)), ((), ()))
LEVELS = 32000.0
CODE_ROWS = 16
RING = 4
AWAY = (1, 3, 2)
NEAR = (1, 3)


def dot(lhs, rhs, dims):
    return lax.dot_general(lhs, rhs, dims, preferred_element_type=jnp.float32)


def split_bf16(value):
    high = value.astype(jnp.bfloat16)
    low = (value - high.astype(jnp.float32)).astype(jnp.bfloat16)
    return high, low


def encode(value, target, row):
    rows = value.shape[0]
    top = jnp.maximum(jnp.max(jnp.abs(value), axis=0, keepdims=True), 1e-30)
    code = jnp.ceil(jnp.log2(top) * 256.0) + 1.0
    scale = LEVELS * jnp.exp2(code * (-1.0 / 256.0))
    target[pl.ds(row, rows), :] = jnp.round(value * scale).astype(jnp.int32).astype(jnp.int16)
    target[pl.ds(row + rows, CODE_ROWS), :] = (
        jnp.broadcast_to(code, (CODE_ROWS, value.shape[1])).astype(jnp.int32).astype(jnp.int16)
    )


def decode(source, row, rows):
    code = source[pl.ds(row + rows, CODE_ROWS), :].astype(jnp.int32).astype(jnp.float32)[0:1, :]
    unit = jnp.exp2(code * (1.0 / 256.0)) * (1.0 / LEVELS)
    return source[pl.ds(row, rows), :].astype(jnp.int32).astype(jnp.float32) * unit


class Sends:
    def __init__(self, send_sems, recv_sems):
        self.send_sems, self.recv_sems = send_sems, recv_sems
        self.count = 0
        self.started = []

    def make(self, source, target, device):
        index = self.count
        self.count += 1
        return pltpu.make_async_remote_copy(
            src_ref=source,
            dst_ref=target,
            send_sem=self.send_sems.at[index],
            recv_sem=self.recv_sems.at[index],
            device_id=device,
            device_id_type=MESH,
        )

    def start(self, source, target, device):
        copy = self.make(source, target, device)
        copy.start()
        self.started.append(copy)
        return copy

    def finish(self):
        for copy in self.started:
            copy.wait_send()


SENDS = 80


def kernel(
    totals,
    tile_pos,
    comp_ref,
    assay_ref,
    bil_ref,
    gc_ref,
    ga_ref,
    gb_ref,
    comps,
    assays,
    query,
    slope,
    pulled,
    grads,
    grads_out,
    grads_in,
    pull_out,
    pull_in,
    pull_z_out,
    pull_z_in,
    grad_out,
    grad_in,
    grad_z_out,
    grad_z_in,
    weight,
    weight_x,
    weight_y,
    weight_z,
    weight_l,
    weight_c,
    send_sems,
    recv_sems,
    local_sems,
):
    total_comp, total_assay, width = totals
    cmp, asy = lax.axis_index("cmp"), lax.axis_index("asy")
    c, zh, y = cmp % 2, (cmp // 2) % RING, cmp // (2 * RING)
    zl, x = asy % 2, asy // 2
    oc, ol = 1 - c, 1 - zl

    def at(y_=None, zh_=None, c_=None, x_=None, zl_=None):
        y_ = y if y_ is None else y_
        zh_ = zh if zh_ is None else zh_
        c_ = c if c_ is None else c_
        x_ = x if x_ is None else x_
        zl_ = zl if zl_ is None else zl_
        return ((y_ * RING + zh_) * 2 + c_, x_ * 2 + zl_)

    def turn(place, step):
        return lax.rem(place + step, RING)

    peer_c = at(c_=oc)
    peer_l = at(zl_=ol)
    peer_x = {d: at(x_=turn(x, d)) for d in AWAY}
    peer_y = {d: at(y_=turn(y, d)) for d in AWAY}
    peer_z = {d: at(zh_=turn(zh, d)) for d in AWAY}
    partners = [*peer_z.values(), *peer_x.values(), *peer_y.values(), peer_l, peer_c]

    rows_c, rows_a = comp_ref.shape[0], assay_ref.shape[0]
    half_c = RING * rows_c

    def x_rows(x_, count=1):
        return pl.ds(pl.multiple_of(x_ * rows_c, rows_c), count * rows_c)

    def comp_rows(h, x_):
        return comps.at[h, x_rows(x_)]

    def assay_rows(zh_, y_):
        return assays.at[zh_, c, pl.ds(y_ * rows_a, rows_a)]

    def make_query(h, x_):
        block = comps[h, x_rows(x_), :]
        query[h, x_rows(x_), :] = dot(block, bil_ref[...], NN).astype(jnp.bfloat16)

    barrier = pltpu.get_barrier_semaphore()
    for partner in partners:
        pl.semaphore_signal(barrier, inc=1, device_id=partner, device_id_type=MESH)
    own_comp = pltpu.make_async_copy(comp_ref, comp_rows(zl, x), local_sems.at[0])
    own_assay = pltpu.make_async_copy(assay_ref, assay_rows(zh, y), local_sems.at[1])
    own_comp.start()
    own_assay.start()
    own_comp.wait()
    own_assay.wait()
    make_query(zl, x)
    pl.semaphore_wait(barrier, len(partners))

    net = Sends(send_sems, recv_sems)

    a_z, c_x, c_f, a_y, a_f, a_c = {}, {}, {}, {}, {}, {}
    c_l = net.start(comp_ref, comp_rows(zl, x), peer_l)
    for d in NEAR:
        a_z[d] = net.start(assay_ref, assay_rows(zh, y), peer_z[d])
    for d in AWAY:
        a_y[d] = net.start(assay_ref, assay_rows(zh, y), peer_y[d])
        c_x[d] = net.start(comp_ref, comp_rows(zl, x), peer_x[d])

    def share(d):
        block = assays.at[turn(zh, RING - d), c]
        a_c[d] = net.start(block, block, peer_c)

    def spread(d):
        a_z[d].wait_recv()
        block = assay_rows(turn(zh, RING - d), y)
        for e in AWAY:
            a_f[d, e] = net.start(block, block, peer_y[e])

    def gathered(d):
        for e in AWAY:
            a_f[d, e].wait_recv()
        share(d)

    scale = 1.0 / math.sqrt(width)

    def score(h, x_, count, s, first=False):
        rows = x_rows(x_, count)
        q = query[h, rows, :] * jnp.bfloat16(scale)
        total = None
        for cc in range(2):
            chunk = assays[s, cc]
            scores = dot(q, chunk, NT)
            sig = 1.0 / (1.0 + jnp.exp(-scores))
            high = []
            for i in range(count):
                wide = []
                for j in range(RING):
                    label = tile_pos[x_ + i, 2 * j + s // 2].astype(jnp.float32)
                    piece = sig[i * rows_c : (i + 1) * rows_c, j * rows_a : (j + 1) * rows_a]
                    wide.append((piece - label).astype(jnp.bfloat16))
                high.append(jnp.concatenate(wide, axis=1))
            part = high[0] if count == 1 else jnp.concatenate(high, axis=0)
            start = pl.multiple_of(h * half_c + x_ * rows_c, rows_c)
            slope[s, cc, pl.ds(start, count * rows_c), :] = part
            term = dot(part, chunk, NN)
            total = term if total is None else total + term
        pulled[h, rows, :] = total if first else pulled[h, rows, :] + total

    def score_all(h, s, first=False):
        for x_ in (0, 2):
            score(h, x_, 2, s, first)

    s0, s1, s3, s2 = zh, turn(zh, 3), turn(zh, 1), turn(zh, 2)
    c_l.wait_recv()
    block = comp_rows(ol, x)
    for d in NEAR:
        c_f[d] = net.start(block, block, peer_x[d])
    spread(1)
    spread(3)
    a_z[2] = net.start(assay_ref, assay_rows(zh, y), peer_z[2])
    for d in AWAY:
        a_y[d].wait_recv()
    share(0)
    c_f[2] = net.start(block, block, peer_x[2])
    make_query(ol, x)
    for d in AWAY:
        c_x[d].wait_recv()
        make_query(zl, turn(x, RING - d))
    a_c[0].wait_recv()
    score_all(zl, s0, True)
    for d in NEAR:
        c_f[d].wait_recv()
        make_query(ol, turn(x, RING - d))
    for d in (0, 1, 3):
        score(ol, turn(x, d), 1, s0, True)
    spread(2)
    gathered(1)
    c_f[2].wait_recv()
    make_query(ol, turn(x, 2))
    score(ol, turn(x, 2), 1, s0, True)
    a_c[1].wait_recv()
    score_all(zl, s1)
    gathered(3)
    score_all(ol, s1)
    a_c[3].wait_recv()
    score_all(zl, s3)
    gathered(2)
    score_all(ol, s3)
    a_c[2].wait_recv()

    p_x = {}

    def send_pulled(i, h):
        for d in (2, 1, 3):
            slot = AWAY.index(d)
            encode(pulled[h, x_rows(turn(x, d)), :], pull_out.at[slot, i], 0)
            p_x[d, i] = net.start(pull_out.at[slot, i], pull_in.at[slot, i], peer_x[d])

    for i, h in enumerate((ol, zl)):
        score_all(h, s2)
        high, low = split_bf16(pulled[h])
        term = dot(comps[h], high, TN) + dot(comps[h], low, TN)
        if i == 0:
            weight[...] = term
            send_pulled(i, h)
        else:
            weight[...] += term

    part_c = width // 2
    part_x = part_c // RING
    part_y = part_x // RING
    w_x, w_y, w_z = {}, {}, {}
    row_c = c * part_c
    row_x = row_c + x * part_x
    row_y = row_x + y * part_y
    w_c = net.start(weight.at[pl.ds(oc * part_c, part_c)], weight_c, peer_c)

    def weight_at_x():
        w_c.wait_recv()
        mine = weight.at[pl.ds(row_c, part_c)]
        mine[...] += weight_c[...]
        for d in AWAY:
            rows = pl.ds(row_c + turn(x, d) * part_x, part_x)
            w_x[d] = net.start(weight.at[rows], weight_x.at[AWAY.index(d)], peer_x[d])

    g_c, g_y, g_z = {}, {}, {}

    def grad(d, own):
        s = turn(zh, d)
        right = query[...].reshape(2 * half_c, width)
        if own:
            grads[s] = dot(slope[s, c], right, TN)
        else:
            grads_out[s] = dot(slope[s, oc], right, TN)
            g_c[d] = net.start(grads_out.at[s], grads_in.at[s], peer_c)

    def send_grad(d):
        s = turn(zh, d)
        g_c[d].wait_recv()
        for e in AWAY:
            slot = AWAY.index(e)
            rows = pl.ds(turn(y, e) * rows_a, rows_a)
            encode(grads[s, rows, :] + grads_in[s, rows, :], grad_out.at[s, slot], 0)
            g_y[d, e] = net.start(grad_out.at[s, slot], grad_in.at[s, slot], peer_y[e])

    def grad_rows(d):
        s = turn(zh, d)
        rows = pl.ds(y * rows_a, rows_a)
        value = grads[s, rows, :] + grads_in[s, rows, :]
        for e in AWAY:
            g_y[d, e].wait_recv()
        for slot in range(3):
            value = value + decode(grad_in.at[s, slot], 0, rows_a)
        return value

    def forward_grad(d):
        slot = AWAY.index(d)
        encode(grad_rows(d), grad_z_out.at[slot], 0)
        g_z[d] = net.start(grad_z_out.at[slot], grad_z_in.at[slot], peer_z[d])

    def pulled_rows(i, h):
        value = pulled[h, x_rows(x), :]
        for d in AWAY:
            p_x[d, i].wait_recv()
        for slot in range(3):
            value = value + decode(pull_in.at[slot, i], 0, rows_c)
        return value

    def weight_at_y():
        for d in AWAY:
            w_x[d].wait_recv()
        mine = weight.at[pl.ds(row_x, part_x)]
        mine[...] = mine[...] + weight_x[0] + weight_x[1] + weight_x[2]
        for d in AWAY:
            rows = pl.ds(row_x + turn(y, d) * part_y, part_y)
            w_y[d] = net.start(weight.at[rows], weight_y.at[AWAY.index(d)], peer_y[d])

    def weight_at_z():
        for d in AWAY:
            w_y[d].wait_recv()
        weight_z[zh] = weight[pl.ds(row_y, part_y), :] + weight_y[0] + weight_y[1] + weight_y[2]
        for d in AWAY:
            w_z[d] = net.start(weight_z.at[zh], weight_z.at[zh], peer_z[d])

    def weight_at_l():
        for d in AWAY:
            w_z[d].wait_recv()
        weight_l[zl] = (weight_z[0] + weight_z[1]) + (weight_z[2] + weight_z[3])
        return net.start(weight_l.at[zl], weight_l.at[zl], peer_l)

    def weight_back(copies, total):
        for copy in copies:
            copy.wait_recv()
        if total:
            gb_ref[pl.ds(row_y, part_y), :] = (weight_l[0] + weight_l[1]) * (
                1.0 / math.sqrt(total_comp * total_assay)
            )

    def spread_back(row, part, devices):
        block = gb_ref.at[pl.ds(row, part)]
        return [net.start(block, block, device) for device in devices]

    grad(2, False)
    weight_at_x()
    grad(2, True)
    grad(1, False)
    send_grad(2)
    weight_at_y()
    send_pulled(1, zl)
    grad(1, True)
    weight_at_z()
    grad(3, False)
    send_grad(1)
    grad(3, True)
    w_l = weight_at_l()
    grad(0, False)
    send_grad(3)
    weight_back([w_l], True)
    w_gy = spread_back(row_y, part_y, [peer_y[d] for d in AWAY])
    grad(0, True)
    send_grad(0)
    weight_back(w_gy, False)
    w_gx = spread_back(row_x, part_x, [peer_x[d] for d in AWAY])
    encode(pulled_rows(0, ol), pull_z_out, 0)
    p_l = net.start(pull_z_out, pull_z_in, peer_l)
    forward_grad(2)
    weight_back(w_gx, False)
    w_gc = spread_back(row_c, part_c, [peer_c])
    forward_grad(1)
    forward_grad(3)
    pulled_own = pulled_rows(1, zl)
    p_l.wait_recv()
    high, low = split_bf16(pulled_own + decode(pull_z_in, 0, rows_c))
    gc_ref[...] = (dot(high, bil_ref[...], NT) + dot(low, bil_ref[...], NT)) * (1.0 / math.sqrt(total_assay))
    grad_own = grad_rows(0)
    for d in AWAY:
        g_z[d].wait_recv()
    for slot in range(3):
        grad_own = grad_own + decode(grad_z_in.at[slot], 0, rows_a)
    ga_ref[...] = grad_own * (1.0 / math.sqrt(total_comp))
    weight_back(w_gc, False)
    net.finish()


def local(comp_emb, assay_emb, bilinear, tile_pos):
    size_cmp, size_asy = lax.axis_size("cmp"), lax.axis_size("asy")
    rows_c, width = comp_emb.shape
    rows_a = assay_emb.shape[0]
    total_comp, total_assay = rows_c * size_cmp * size_asy, rows_a * size_cmp * size_asy
    half_c, group_a = rows_c * RING, rows_a * RING
    part = width // 2 // RING
    vmem = pl.BlockSpec(memory_space=pltpu.VMEM)
    block_c, block_a = rows_c + CODE_ROWS, rows_a + CODE_ROWS
    return tuple(
        pl.pallas_call(
            functools.partial(kernel, (total_comp, total_assay, width)),
            out_shape=[
                jax.ShapeDtypeStruct((rows_c, width), jnp.float32),
                jax.ShapeDtypeStruct((rows_a, width), jnp.float32),
                jax.ShapeDtypeStruct((width, width), jnp.float32),
            ],
            in_specs=[
                pl.BlockSpec(memory_space=pltpu.SMEM),
                pl.BlockSpec(memory_space=pl.ANY),
                pl.BlockSpec(memory_space=pl.ANY),
                vmem,
            ],
            out_specs=[vmem, vmem, vmem],
            scratch_shapes=[
                pltpu.VMEM((2, half_c, width), jnp.bfloat16),
                pltpu.VMEM((RING, 2, group_a, width), jnp.bfloat16),
                pltpu.VMEM((2, half_c, width), jnp.bfloat16),
                pltpu.VMEM((RING, 2, 2 * half_c, group_a), jnp.bfloat16),
                pltpu.VMEM((2, half_c, width), jnp.float32),
                pltpu.VMEM((RING, group_a, width), jnp.float32),
                pltpu.VMEM((RING, group_a, width), jnp.float32),
                pltpu.VMEM((RING, group_a, width), jnp.float32),
                pltpu.VMEM((3, 2, block_c, width), jnp.int16),
                pltpu.VMEM((3, 2, block_c, width), jnp.int16),
                pltpu.VMEM((block_c, width), jnp.int16),
                pltpu.VMEM((block_c, width), jnp.int16),
                pltpu.VMEM((RING, 3, block_a, width), jnp.int16),
                pltpu.VMEM((RING, 3, block_a, width), jnp.int16),
                pltpu.VMEM((3, block_a, width), jnp.int16),
                pltpu.VMEM((3, block_a, width), jnp.int16),
                pltpu.VMEM((width, width), jnp.float32),
                pltpu.VMEM((3, part, width), jnp.float32),
                pltpu.VMEM((3, part // RING, width), jnp.float32),
                pltpu.VMEM((RING, part // RING, width), jnp.float32),
                pltpu.VMEM((2, part // RING, width), jnp.float32),
                pltpu.VMEM((width // 2, width), jnp.float32),
                pltpu.SemaphoreType.DMA((SENDS,)),
                pltpu.SemaphoreType.DMA((SENDS,)),
                pltpu.SemaphoreType.DMA((2,)),
            ],
            compiler_params=pltpu.CompilerParams(
                collective_id=0, has_side_effects=True, vmem_limit_bytes=58 * 2**20
            ),
            name="link_grads",
        )(tile_pos, comp_emb, assay_emb, bilinear)
    )


def solution(mesh):
    return jax.shard_map(
        local,
        mesh=mesh,
        in_specs=(P(("cmp", "asy"), None), P(("asy", "cmp"), None), P(), P("cmp", "asy")),
        out_specs=(P(("cmp", "asy"), None), P(("asy", "cmp"), None), P()),
        check_vma=False,
    )
```

```python
import functools
import math

import jax
import jax.numpy as jnp
from jax import lax
from jax.experimental import pallas as pl
from jax.experimental.pallas import tpu as pltpu
from jax.sharding import PartitionSpec as P

MESH = pl.DeviceIdType.MESH
NN = (((1,), (0,)), ((), ()))
NT = (((1,), (1,)), ((), ()))
TN = (((0,), (0,)), ((), ()))
LEVELS = 32000.0
CODE_ROWS = 16
RING = 4
AWAY = (1, 3, 2)
NEAR = (1, 3)


def dot(lhs, rhs, dims):
    return lax.dot_general(lhs, rhs, dims, preferred_element_type=jnp.float32)


def split_bf16(value):
    high = value.astype(jnp.bfloat16)
    low = (value - high.astype(jnp.float32)).astype(jnp.bfloat16)
    return high, low


def encode(value, target, row):
    rows = value.shape[0]
    top = jnp.maximum(jnp.max(jnp.abs(value), axis=0, keepdims=True), 1e-30)
    code = jnp.ceil(jnp.log2(top) * 256.0) + 1.0
    scale = LEVELS * jnp.exp2(code * (-1.0 / 256.0))
    target[pl.ds(row, rows), :] = jnp.round(value * scale).astype(jnp.int32).astype(jnp.int16)
    target[pl.ds(row + rows, CODE_ROWS), :] = (
        jnp.broadcast_to(code, (CODE_ROWS, value.shape[1])).astype(jnp.int32).astype(jnp.int16)
    )


def decode(source, row, rows):
    code = source[pl.ds(row + rows, CODE_ROWS), :].astype(jnp.int32).astype(jnp.float32)[0:1, :]
    unit = jnp.exp2(code * (1.0 / 256.0)) * (1.0 / LEVELS)
    return source[pl.ds(row, rows), :].astype(jnp.int32).astype(jnp.float32) * unit


class Sends:
    def __init__(self, send_sems, recv_sems):
        self.send_sems, self.recv_sems = send_sems, recv_sems
        self.count = 0
        self.started = []

    def make(self, source, target, device):
        index = self.count
        self.count += 1
        return pltpu.make_async_remote_copy(
            src_ref=source,
            dst_ref=target,
            send_sem=self.send_sems.at[index],
            recv_sem=self.recv_sems.at[index],
            device_id=device,
            device_id_type=MESH,
        )

    def start(self, source, target, device):
        copy = self.make(source, target, device)
        copy.start()
        self.started.append(copy)
        return copy

    def finish(self):
        for copy in self.started:
            copy.wait_send()


SENDS = 80


def kernel(
    totals,
    tile_pos,
    comp_ref,
    assay_ref,
    bil_ref,
    gc_ref,
    ga_ref,
    gb_ref,
    comps,
    assays,
    query,
    slope,
    pulled,
    grads,
    grads_out,
    grads_in,
    pull_out,
    pull_in,
    pull_z_out,
    pull_z_in,
    grad_out,
    grad_in,
    grad_z_out,
    grad_z_in,
    weight,
    weight_x,
    weight_y,
    weight_z,
    weight_l,
    weight_c,
    send_sems,
    recv_sems,
    local_sems,
):
    width = totals[2]
    cmp, asy = lax.axis_index("cmp"), lax.axis_index("asy")
    c, zh, y = cmp % 2, (cmp // 2) % RING, cmp // (2 * RING)
    zl, x = asy % 2, asy // 2
    oc, ol = 1 - c, 1 - zl

    def at(y_=None, zh_=None, c_=None, x_=None, zl_=None):
        y_ = y if y_ is None else y_
        zh_ = zh if zh_ is None else zh_
        c_ = c if c_ is None else c_
        x_ = x if x_ is None else x_
        zl_ = zl if zl_ is None else zl_
        return ((y_ * RING + zh_) * 2 + c_, x_ * 2 + zl_)

    def turn(place, step):
        return lax.rem(place + step, RING)

    peer_c = at(c_=oc)
    peer_l = at(zl_=ol)
    peer_x = {d: at(x_=turn(x, d)) for d in AWAY}
    peer_y = {d: at(y_=turn(y, d)) for d in AWAY}
    peer_z = {d: at(zh_=turn(zh, d)) for d in AWAY}
    partners = [*peer_z.values(), *peer_x.values(), *peer_y.values(), peer_l, peer_c]

    rows_c, rows_a = comp_ref.shape[0], assay_ref.shape[0]
    half_c = RING * rows_c

    def x_rows(x_, count=1):
        return pl.ds(pl.multiple_of(x_ * rows_c, rows_c), count * rows_c)

    def comp_rows(h, x_):
        return comps.at[h, x_rows(x_)]

    def assay_rows(zh_, y_):
        return assays.at[zh_, c, pl.ds(y_ * rows_a, rows_a)]

    def make_query(h, x_):
        block = comps[h, x_rows(x_), :]
        query[h, x_rows(x_), :] = dot(block, bil_ref[...], NN).astype(jnp.bfloat16)

    barrier = pltpu.get_barrier_semaphore()
    for partner in partners:
        pl.semaphore_signal(barrier, inc=1, device_id=partner, device_id_type=MESH)
    own_comp = pltpu.make_async_copy(comp_ref, comp_rows(zl, x), local_sems.at[0])
    own_assay = pltpu.make_async_copy(assay_ref, assay_rows(zh, y), local_sems.at[1])
    own_comp.start()
    own_assay.start()
    own_comp.wait()
    own_assay.wait()
    make_query(zl, x)
    pl.semaphore_wait(barrier, len(partners))

    net = Sends(send_sems, recv_sems)

    a_z, c_x, c_f, a_y, a_f, a_c = {}, {}, {}, {}, {}, {}
    c_l = net.start(comp_ref, comp_rows(zl, x), peer_l)
    for d in NEAR:
        a_z[d] = net.start(assay_ref, assay_rows(zh, y), peer_z[d])
    for d in AWAY:
        a_y[d] = net.start(assay_ref, assay_rows(zh, y), peer_y[d])
        c_x[d] = net.start(comp_ref, comp_rows(zl, x), peer_x[d])

    def share(d):
        block = assays.at[turn(zh, RING - d), c]
        a_c[d] = net.start(block, block, peer_c)

    def spread(d):
        a_z[d].wait_recv()
        block = assay_rows(turn(zh, RING - d), y)
        for e in AWAY:
            a_f[d, e] = net.start(block, block, peer_y[e])

    def gathered(d):
        for e in AWAY:
            a_f[d, e].wait_recv()
        share(d)

    scale = 1.0 / math.sqrt(width)

    def score(h, x_, count, s, first=False):
        rows = x_rows(x_, count)
        q = query[h, rows, :] * jnp.bfloat16(scale)
        total = None
        for cc in range(2):
            chunk = assays[s, cc]
            scores = dot(q, chunk, NT)
            sig = 1.0 / (1.0 + jnp.exp(-scores))
            high = []
            for i in range(count):
                wide = []
                for j in range(RING):
                    label = tile_pos[x_ + i, 2 * j + s // 2].astype(jnp.float32)
                    piece = sig[i * rows_c : (i + 1) * rows_c, j * rows_a : (j + 1) * rows_a]
                    wide.append((piece - label).astype(jnp.bfloat16))
                high.append(jnp.concatenate(wide, axis=1))
            part = high[0] if count == 1 else jnp.concatenate(high, axis=0)
            start = pl.multiple_of(h * half_c + x_ * rows_c, rows_c)
            slope[s, cc, pl.ds(start, count * rows_c), :] = part
            term = dot(part, chunk, NN)
            total = term if total is None else total + term
        pulled[h, rows, :] = total if first else pulled[h, rows, :] + total

    def score_all(h, s, first=False):
        for x_ in (0, 2):
            score(h, x_, 2, s, first)

    g_c, g_y, g_z = {}, {}, {}

    def grad(d, own):
        s = turn(zh, d)
        right = query[...].reshape(2 * half_c, width)
        if own:
            grads[s] = dot(slope[s, c], right, TN)
        else:
            grads_out[s] = dot(slope[s, oc], right, TN)
            g_c[d] = net.start(grads_out.at[s], grads_in.at[s], peer_c)

    def send_grad(d):
        s = turn(zh, d)
        g_c[d].wait_recv()
        for e in AWAY:
            slot = AWAY.index(e)
            rows = pl.ds(turn(y, e) * rows_a, rows_a)
            encode(grads[s, rows, :] + grads_in[s, rows, :], grad_out.at[s, slot], 0)
            g_y[d, e] = net.start(grad_out.at[s, slot], grad_in.at[s, slot], peer_y[e])

    def grad_rows(d):
        s = turn(zh, d)
        rows = pl.ds(y * rows_a, rows_a)
        value = grads[s, rows, :] + grads_in[s, rows, :]
        for e in AWAY:
            g_y[d, e].wait_recv()
        for slot in range(3):
            value = value + decode(grad_in.at[s, slot], 0, rows_a)
        return value

    def forward_grad(d):
        slot = AWAY.index(d)
        encode(grad_rows(d), grad_z_out.at[slot], 0)
        g_z[d] = net.start(grad_z_out.at[slot], grad_z_in.at[slot], peer_z[d])

    s0, s1, s3, s2 = zh, turn(zh, 3), turn(zh, 1), turn(zh, 2)
    c_l.wait_recv()
    block = comp_rows(ol, x)
    for d in NEAR:
        c_f[d] = net.start(block, block, peer_x[d])
    spread(1)
    spread(3)
    a_z[2] = net.start(assay_ref, assay_rows(zh, y), peer_z[2])
    for d in AWAY:
        a_y[d].wait_recv()
    share(0)
    c_f[2] = net.start(block, block, peer_x[2])
    make_query(ol, x)
    for d in AWAY:
        c_x[d].wait_recv()
        make_query(zl, turn(x, RING - d))
    a_c[0].wait_recv()
    score_all(zl, s0, True)
    for d in NEAR:
        c_f[d].wait_recv()
        make_query(ol, turn(x, RING - d))
    for d in (0, 1, 3):
        score(ol, turn(x, d), 1, s0, True)
    spread(2)
    gathered(1)
    c_f[2].wait_recv()
    make_query(ol, turn(x, 2))
    score(ol, turn(x, 2), 1, s0, True)
    a_c[1].wait_recv()
    score_all(zl, s1)
    gathered(3)
    score_all(ol, s1)
    grad(3, False)
    a_c[3].wait_recv()
    score_all(zl, s3)
    grad(3, True)
    gathered(2)
    send_grad(3)
    score_all(ol, s3)
    grad(1, False)
    grad(1, True)
    a_c[2].wait_recv()

    p_x = {}

    def send_pulled(i, h):
        for d in (2, 1, 3):
            slot = AWAY.index(d)
            encode(pulled[h, x_rows(turn(x, d)), :], pull_out.at[slot, i], 0)
            p_x[d, i] = net.start(pull_out.at[slot, i], pull_in.at[slot, i], peer_x[d])

    for i, h in enumerate((ol, zl)):
        score_all(h, s2)
        if i == 0:
            send_grad(1)
        high, low = split_bf16(pulled[h])
        term = dot(comps[h], high, TN) + dot(comps[h], low, TN)
        if i == 0:
            weight[...] = term
            send_pulled(i, h)
        else:
            weight[...] += term

    part_c = width // 2
    part_x = part_c // RING
    part_y = part_x // RING
    w_x, w_y, w_z = {}, {}, {}
    row_c = c * part_c
    row_x = row_c + x * part_x
    row_y = row_x + y * part_y
    w_c = net.start(weight.at[pl.ds(oc * part_c, part_c)], weight_c, peer_c)

    def weight_at_x():
        w_c.wait_recv()
        mine = weight.at[pl.ds(row_c, part_c)]
        mine[...] += weight_c[...]
        for d in AWAY:
            rows = pl.ds(row_c + turn(x, d) * part_x, part_x)
            w_x[d] = net.start(weight.at[rows], weight_x.at[AWAY.index(d)], peer_x[d])

    def pulled_rows(i, h):
        value = pulled[h, x_rows(x), :]
        for d in AWAY:
            p_x[d, i].wait_recv()
        for slot in range(3):
            value = value + decode(pull_in.at[slot, i], 0, rows_c)
        return value

    def weight_at_y():
        for d in AWAY:
            w_x[d].wait_recv()
        mine = weight.at[pl.ds(row_x, part_x)]
        mine[...] = mine[...] + weight_x[0] + weight_x[1] + weight_x[2]
        for d in AWAY:
            rows = pl.ds(row_x + turn(y, d) * part_y, part_y)
            w_y[d] = net.start(weight.at[rows], weight_y.at[AWAY.index(d)], peer_y[d])

    def weight_at_z():
        for d in AWAY:
            w_y[d].wait_recv()
        weight_z[zh] = weight[pl.ds(row_y, part_y), :] + weight_y[0] + weight_y[1] + weight_y[2]
        for d in AWAY:
            w_z[d] = net.start(weight_z.at[zh], weight_z.at[zh], peer_z[d])

    def weight_at_l():
        for d in AWAY:
            w_z[d].wait_recv()
        weight_l[zl] = (weight_z[0] + weight_z[1]) + (weight_z[2] + weight_z[3])
        return net.start(weight_l.at[zl], weight_l.at[zl], peer_l)

    def weight_back(copies, total):
        for copy in copies:
            copy.wait_recv()
        if total:
            gb_ref[pl.ds(row_y, part_y), :] = weight_l[0] + weight_l[1]

    def spread_back(row, part, devices):
        block = gb_ref.at[pl.ds(row, part)]
        return [net.start(block, block, device) for device in devices]

    grad(2, False)
    weight_at_x()
    grad(2, True)
    send_grad(2)
    forward_grad(3)
    grad(0, False)
    weight_at_y()
    send_pulled(1, zl)
    grad(0, True)
    weight_at_z()
    send_grad(0)
    forward_grad(1)
    w_l = weight_at_l()
    encode(pulled_rows(0, ol), pull_z_out, 0)
    p_l = net.start(pull_z_out, pull_z_in, peer_l)
    weight_back([w_l], True)
    w_gy = spread_back(row_y, part_y, [peer_y[d] for d in AWAY])
    forward_grad(2)
    weight_back(w_gy, False)
    w_gx = spread_back(row_x, part_x, [peer_x[d] for d in AWAY])
    pulled_own = pulled_rows(1, zl)
    p_l.wait_recv()
    high, low = split_bf16(pulled_own + decode(pull_z_in, 0, rows_c))
    gc_ref[...] = dot(high, bil_ref[...], NT) + dot(low, bil_ref[...], NT)
    weight_back(w_gx, False)
    w_gc = spread_back(row_c, part_c, [peer_c])
    grad_own = grad_rows(0)
    for d in AWAY:
        g_z[d].wait_recv()
    for slot in range(3):
        grad_own = grad_own + decode(grad_z_in.at[slot], 0, rows_a)
    ga_ref[...] = grad_own
    weight_back(w_gc, False)
    net.finish()


def scale_kernel(totals, gc_in, ga_in, gb_in, gc_ref, ga_ref, gb_ref):
    total_comp, total_assay, _ = totals
    gc_ref[...] = gc_in[...] * (1.0 / math.sqrt(total_assay))
    ga_ref[...] = ga_in[...] * (1.0 / math.sqrt(total_comp))
    gb_ref[...] = gb_in[...] * (1.0 / math.sqrt(total_comp * total_assay))


def local(comp_emb, assay_emb, bilinear, tile_pos):
    size_cmp, size_asy = lax.axis_size("cmp"), lax.axis_size("asy")
    rows_c, width = comp_emb.shape
    rows_a = assay_emb.shape[0]
    total_comp, total_assay = rows_c * size_cmp * size_asy, rows_a * size_cmp * size_asy
    half_c, group_a = rows_c * RING, rows_a * RING
    part = width // 2 // RING
    vmem = pl.BlockSpec(memory_space=pltpu.VMEM)
    block_c, block_a = rows_c + CODE_ROWS, rows_a + CODE_ROWS
    totals = (total_comp, total_assay, width)
    shapes = [
        jax.ShapeDtypeStruct((rows_c, width), jnp.float32),
        jax.ShapeDtypeStruct((rows_a, width), jnp.float32),
        jax.ShapeDtypeStruct((width, width), jnp.float32),
    ]
    sums = (
        pl.pallas_call(
            functools.partial(kernel, totals),
            out_shape=shapes,
            in_specs=[
                pl.BlockSpec(memory_space=pltpu.SMEM),
                pl.BlockSpec(memory_space=pl.ANY),
                pl.BlockSpec(memory_space=pl.ANY),
                vmem,
            ],
            out_specs=[vmem, vmem, vmem],
            scratch_shapes=[
                pltpu.VMEM((2, half_c, width), jnp.bfloat16),
                pltpu.VMEM((RING, 2, group_a, width), jnp.bfloat16),
                pltpu.VMEM((2, half_c, width), jnp.bfloat16),
                pltpu.VMEM((RING, 2, 2 * half_c, group_a), jnp.bfloat16),
                pltpu.VMEM((2, half_c, width), jnp.float32),
                pltpu.VMEM((RING, group_a, width), jnp.float32),
                pltpu.VMEM((RING, group_a, width), jnp.float32),
                pltpu.VMEM((RING, group_a, width), jnp.float32),
                pltpu.VMEM((3, 2, block_c, width), jnp.int16),
                pltpu.VMEM((3, 2, block_c, width), jnp.int16),
                pltpu.VMEM((block_c, width), jnp.int16),
                pltpu.VMEM((block_c, width), jnp.int16),
                pltpu.VMEM((RING, 3, block_a, width), jnp.int16),
                pltpu.VMEM((RING, 3, block_a, width), jnp.int16),
                pltpu.VMEM((3, block_a, width), jnp.int16),
                pltpu.VMEM((3, block_a, width), jnp.int16),
                pltpu.VMEM((width, width), jnp.float32),
                pltpu.VMEM((3, part, width), jnp.float32),
                pltpu.VMEM((3, part // RING, width), jnp.float32),
                pltpu.VMEM((RING, part // RING, width), jnp.float32),
                pltpu.VMEM((2, part // RING, width), jnp.float32),
                pltpu.VMEM((width // 2, width), jnp.float32),
                pltpu.SemaphoreType.DMA((SENDS,)),
                pltpu.SemaphoreType.DMA((SENDS,)),
                pltpu.SemaphoreType.DMA((2,)),
            ],
            compiler_params=pltpu.CompilerParams(
                collective_id=0, has_side_effects=True, vmem_limit_bytes=58 * 2**20
            ),
            name="link_grads",
        )(tile_pos, comp_emb, assay_emb, bilinear)
    )
    return tuple(
        pl.pallas_call(
            functools.partial(scale_kernel, totals),
            out_shape=shapes,
            in_specs=[vmem, vmem, vmem],
            out_specs=[vmem, vmem, vmem],
            name="scale_grads",
        )(*sums)
    )


def solution(mesh):
    return jax.shard_map(
        local,
        mesh=mesh,
        in_specs=(P(("cmp", "asy"), None), P(("asy", "cmp"), None), P(), P("cmp", "asy")),
        out_specs=(P(("cmp", "asy"), None), P(("asy", "cmp"), None), P()),
        check_vma=False,
    )
```

```python
import functools
import math

import jax
import jax.numpy as jnp
from jax import lax
from jax.experimental import pallas as pl
from jax.experimental.pallas import tpu as pltpu
from jax.sharding import PartitionSpec as P

MESH = pl.DeviceIdType.MESH
NN = (((1,), (0,)), ((), ()))
NT = (((1,), (1,)), ((), ()))
TN = (((0,), (0,)), ((), ()))
LEVELS = 32000.0
CODE_ROWS = 16
RING = 4
AWAY = (1, 3, 2)
NEAR = (1, 3)


def dot(lhs, rhs, dims):
    return lax.dot_general(lhs, rhs, dims, preferred_element_type=jnp.float32)


def split_bf16(value):
    high = value.astype(jnp.bfloat16)
    low = (value - high.astype(jnp.float32)).astype(jnp.bfloat16)
    return high, low


def encode(value, target, row):
    rows = value.shape[0]
    top = jnp.maximum(jnp.max(jnp.abs(value), axis=0, keepdims=True), 1e-30)
    code = jnp.ceil(jnp.log2(top) * 256.0) + 1.0
    scale = LEVELS * jnp.exp2(code * (-1.0 / 256.0))
    target[pl.ds(row, rows), :] = jnp.round(value * scale).astype(jnp.int32).astype(jnp.int16)
    target[pl.ds(row + rows, CODE_ROWS), :] = (
        jnp.broadcast_to(code, (CODE_ROWS, value.shape[1])).astype(jnp.int32).astype(jnp.int16)
    )


def decode(source, row, rows):
    code = source[pl.ds(row + rows, CODE_ROWS), :].astype(jnp.int32).astype(jnp.float32)[0:1, :]
    unit = jnp.exp2(code * (1.0 / 256.0)) * (1.0 / LEVELS)
    return source[pl.ds(row, rows), :].astype(jnp.int32).astype(jnp.float32) * unit


class Sends:
    def __init__(self, send_sems, recv_sems):
        self.send_sems, self.recv_sems = send_sems, recv_sems
        self.count = 0
        self.started = []

    def make(self, source, target, device):
        index = self.count
        self.count += 1
        return pltpu.make_async_remote_copy(
            src_ref=source,
            dst_ref=target,
            send_sem=self.send_sems.at[index],
            recv_sem=self.recv_sems.at[index],
            device_id=device,
            device_id_type=MESH,
        )

    def start(self, source, target, device):
        copy = self.make(source, target, device)
        copy.start()
        self.started.append(copy)
        return copy

    def finish(self):
        for copy in self.started:
            copy.wait_send()


SENDS = 80


def kernel(
    totals,
    tile_pos,
    comp_ref,
    assay_ref,
    bil_ref,
    gc_ref,
    ga_ref,
    gb_ref,
    comps,
    assays,
    query,
    slope,
    pulled,
    grads,
    grads_out,
    grads_in,
    pull_out,
    pull_in,
    pull_z_out,
    pull_z_in,
    grad_out,
    grad_in,
    grad_z_out,
    grad_z_in,
    weight,
    weight_x,
    weight_y,
    weight_z,
    weight_l,
    weight_c,
    send_sems,
    recv_sems,
    local_sems,
):
    width = totals[2]
    cmp, asy = lax.axis_index("cmp"), lax.axis_index("asy")
    c, zh, y = cmp % 2, (cmp // 2) % RING, cmp // (2 * RING)
    zl, x = asy % 2, asy // 2
    oc, ol = 1 - c, 1 - zl

    def at(y_=None, zh_=None, c_=None, x_=None, zl_=None):
        y_ = y if y_ is None else y_
        zh_ = zh if zh_ is None else zh_
        c_ = c if c_ is None else c_
        x_ = x if x_ is None else x_
        zl_ = zl if zl_ is None else zl_
        return ((y_ * RING + zh_) * 2 + c_, x_ * 2 + zl_)

    def turn(place, step):
        return lax.rem(place + step, RING)

    peer_c = at(c_=oc)
    peer_l = at(zl_=ol)
    peer_x = {d: at(x_=turn(x, d)) for d in AWAY}
    peer_y = {d: at(y_=turn(y, d)) for d in AWAY}
    peer_z = {d: at(zh_=turn(zh, d)) for d in AWAY}
    partners = [*peer_z.values(), *peer_x.values(), *peer_y.values(), peer_l, peer_c]

    rows_c, rows_a = comp_ref.shape[0], assay_ref.shape[0]
    half_c = RING * rows_c

    def x_rows(x_, count=1):
        return pl.ds(pl.multiple_of(x_ * rows_c, rows_c), count * rows_c)

    def comp_rows(h, x_):
        return comps.at[h, x_rows(x_)]

    def assay_rows(zh_, y_):
        return assays.at[zh_, c, pl.ds(y_ * rows_a, rows_a)]

    def make_query(h, x_):
        block = comps[h, x_rows(x_), :]
        query[h, x_rows(x_), :] = dot(block, bil_ref[...], NN).astype(jnp.bfloat16)

    barrier = pltpu.get_barrier_semaphore()
    for partner in partners:
        pl.semaphore_signal(barrier, inc=1, device_id=partner, device_id_type=MESH)
    own_comp = pltpu.make_async_copy(comp_ref, comp_rows(zl, x), local_sems.at[0])
    own_assay = pltpu.make_async_copy(assay_ref, assay_rows(zh, y), local_sems.at[1])
    own_comp.start()
    own_assay.start()
    own_comp.wait()
    own_assay.wait()
    make_query(zl, x)
    pl.semaphore_wait(barrier, len(partners))

    net = Sends(send_sems, recv_sems)

    a_z, c_x, c_f, a_y, a_f, a_c = {}, {}, {}, {}, {}, {}
    c_l = net.start(comp_ref, comp_rows(zl, x), peer_l)
    for d in NEAR:
        a_z[d] = net.start(assay_ref, assay_rows(zh, y), peer_z[d])
    for d in AWAY:
        a_y[d] = net.start(assay_ref, assay_rows(zh, y), peer_y[d])
        c_x[d] = net.start(comp_ref, comp_rows(zl, x), peer_x[d])

    def share(d):
        block = assays.at[turn(zh, RING - d), c]
        a_c[d] = net.start(block, block, peer_c)

    def spread(d):
        a_z[d].wait_recv()
        block = assay_rows(turn(zh, RING - d), y)
        for e in AWAY:
            a_f[d, e] = net.start(block, block, peer_y[e])

    def gathered(d):
        for e in AWAY:
            a_f[d, e].wait_recv()
        share(d)

    scale = 1.0 / math.sqrt(width)

    def score(h, x_, count, s, first=False):
        rows = x_rows(x_, count)
        q = query[h, rows, :] * jnp.bfloat16(scale)
        total = None
        for cc in range(2):
            chunk = assays[s, cc]
            scores = dot(q, chunk, NT)
            sig = 1.0 / (1.0 + jnp.exp(-scores))
            high = []
            for i in range(count):
                wide = []
                for j in range(RING):
                    label = tile_pos[x_ + i, 2 * j + s // 2].astype(jnp.float32)
                    piece = sig[i * rows_c : (i + 1) * rows_c, j * rows_a : (j + 1) * rows_a]
                    wide.append((piece - label).astype(jnp.bfloat16))
                high.append(jnp.concatenate(wide, axis=1))
            part = high[0] if count == 1 else jnp.concatenate(high, axis=0)
            start = pl.multiple_of(h * half_c + x_ * rows_c, rows_c)
            slope[s, cc, pl.ds(start, count * rows_c), :] = part
            term = dot(part, chunk, NN)
            total = term if total is None else total + term
        pulled[h, rows, :] = total if first else pulled[h, rows, :] + total

    def score_all(h, s, first=False):
        for x_ in (0, 2):
            score(h, x_, 2, s, first)

    g_c, g_y, g_z = {}, {}, {}

    def grad(d, own):
        s = turn(zh, d)
        right = query[...].reshape(2 * half_c, width)
        if own:
            grads[s] = dot(slope[s, c], right, TN)
        else:
            grads_out[s] = dot(slope[s, oc], right, TN)
            g_c[d] = net.start(grads_out.at[s], grads_in.at[s], peer_c)

    def send_grad(d):
        s = turn(zh, d)
        g_c[d].wait_recv()
        for e in AWAY:
            slot = AWAY.index(e)
            rows = pl.ds(turn(y, e) * rows_a, rows_a)
            encode(grads[s, rows, :] + grads_in[s, rows, :], grad_out.at[s, slot], 0)
            g_y[d, e] = net.start(grad_out.at[s, slot], grad_in.at[s, slot], peer_y[e])

    def grad_rows(d):
        s = turn(zh, d)
        rows = pl.ds(y * rows_a, rows_a)
        value = grads[s, rows, :] + grads_in[s, rows, :]
        for e in AWAY:
            g_y[d, e].wait_recv()
        for slot in range(3):
            value = value + decode(grad_in.at[s, slot], 0, rows_a)
        return value

    def forward_grad(d):
        slot = AWAY.index(d)
        encode(grad_rows(d), grad_z_out.at[slot], 0)
        g_z[d] = net.start(grad_z_out.at[slot], grad_z_in.at[slot], peer_z[d])

    s0, s1, s3, s2 = zh, turn(zh, 3), turn(zh, 1), turn(zh, 2)
    c_l.wait_recv()
    block = comp_rows(ol, x)
    for d in NEAR:
        c_f[d] = net.start(block, block, peer_x[d])
    spread(1)
    spread(3)
    a_z[2] = net.start(assay_ref, assay_rows(zh, y), peer_z[2])
    for d in AWAY:
        a_y[d].wait_recv()
    share(0)
    c_f[2] = net.start(block, block, peer_x[2])
    make_query(ol, x)
    for d in AWAY:
        c_x[d].wait_recv()
        make_query(zl, turn(x, RING - d))
    a_c[0].wait_recv()
    score_all(zl, s0, True)
    for d in NEAR:
        c_f[d].wait_recv()
        make_query(ol, turn(x, RING - d))
    for d in (0, 1, 3):
        score(ol, turn(x, d), 1, s0, True)
    spread(2)
    gathered(1)
    c_f[2].wait_recv()
    make_query(ol, turn(x, 2))
    score(ol, turn(x, 2), 1, s0, True)
    a_c[1].wait_recv()
    score_all(zl, s1)
    gathered(3)
    score_all(ol, s1)
    grad(3, False)
    a_c[3].wait_recv()
    score_all(zl, s3)
    grad(3, True)
    gathered(2)
    send_grad(3)
    score_all(ol, s3)
    grad(1, False)
    grad(1, True)
    a_c[2].wait_recv()

    p_x = {}

    def send_pulled(i, h):
        for d in (2, 1, 3):
            slot = AWAY.index(d)
            encode(pulled[h, x_rows(turn(x, d)), :], pull_out.at[slot, i], 0)
            p_x[d, i] = net.start(pull_out.at[slot, i], pull_in.at[slot, i], peer_x[d])

    for i, h in enumerate((ol, zl)):
        score_all(h, s2)
        if i == 0:
            send_grad(1)
        high, low = split_bf16(pulled[h])
        term = dot(comps[h], high, TN) + dot(comps[h], low, TN)
        if i == 0:
            weight[...] = term
            send_pulled(i, h)
        else:
            weight[...] += term

    part_c = width // 2
    part_x = part_c // RING
    part_y = part_x // RING
    w_x, w_y, w_z = {}, {}, {}
    row_c = c * part_c
    row_x = row_c + x * part_x
    row_y = row_x + y * part_y
    w_c = net.start(weight.at[pl.ds(oc * part_c, part_c)], weight_c, peer_c)

    def weight_at_x():
        w_c.wait_recv()
        mine = weight.at[pl.ds(row_c, part_c)]
        mine[...] += weight_c[...]
        for d in AWAY:
            rows = pl.ds(row_c + turn(x, d) * part_x, part_x)
            w_x[d] = net.start(weight.at[rows], weight_x.at[AWAY.index(d)], peer_x[d])

    def pulled_rows(i, h):
        value = pulled[h, x_rows(x), :]
        for d in AWAY:
            p_x[d, i].wait_recv()
        for slot in range(3):
            value = value + decode(pull_in.at[slot, i], 0, rows_c)
        return value

    def weight_at_y():
        for d in AWAY:
            w_x[d].wait_recv()
        mine = weight.at[pl.ds(row_x, part_x)]
        mine[...] = mine[...] + weight_x[0] + weight_x[1] + weight_x[2]
        for d in AWAY:
            rows = pl.ds(row_x + turn(y, d) * part_y, part_y)
            w_y[d] = net.start(weight.at[rows], weight_y.at[AWAY.index(d)], peer_y[d])

    def weight_at_z():
        for d in AWAY:
            w_y[d].wait_recv()
        weight_z[zh] = weight[pl.ds(row_y, part_y), :] + weight_y[0] + weight_y[1] + weight_y[2]
        for d in AWAY:
            w_z[d] = net.start(weight_z.at[zh], weight_z.at[zh], peer_z[d])

    def weight_at_l():
        for d in AWAY:
            w_z[d].wait_recv()
        weight_l[zl] = (weight_z[0] + weight_z[1]) + (weight_z[2] + weight_z[3])
        return net.start(weight_l.at[zl], weight_l.at[zl], peer_l)

    def weight_back(copies, total):
        for copy in copies:
            copy.wait_recv()
        if total:
            gb_ref[pl.ds(row_y, part_y), :] = weight_l[0] + weight_l[1]

    def spread_back(row, part, devices):
        block = gb_ref.at[pl.ds(row, part)]
        return [net.start(block, block, device) for device in devices]

    grad(2, False)
    weight_at_x()
    send_pulled(1, zl)
    grad(2, True)
    send_grad(2)
    forward_grad(3)
    grad(0, False)
    weight_at_y()
    grad(0, True)
    weight_at_z()
    send_grad(0)
    forward_grad(1)
    w_l = weight_at_l()
    encode(pulled_rows(0, ol), pull_z_out, 0)
    p_l = net.start(pull_z_out, pull_z_in, peer_l)
    weight_back([w_l], True)
    w_gy = spread_back(row_y, part_y, [peer_y[d] for d in AWAY])
    forward_grad(2)
    weight_back(w_gy, False)
    w_gx = spread_back(row_x, part_x, [peer_x[d] for d in AWAY])
    pulled_own = pulled_rows(1, zl)
    p_l.wait_recv()
    high, low = split_bf16(pulled_own + decode(pull_z_in, 0, rows_c))
    gc_ref[...] = dot(high, bil_ref[...], NT) + dot(low, bil_ref[...], NT)
    weight_back(w_gx, False)
    w_gc = spread_back(row_c, part_c, [peer_c])
    grad_own = grad_rows(0)
    for d in AWAY:
        g_z[d].wait_recv()
    for slot in range(3):
        grad_own = grad_own + decode(grad_z_in.at[slot], 0, rows_a)
    ga_ref[...] = grad_own
    weight_back(w_gc, False)
    net.finish()


def scale_kernel(totals, gc_in, ga_in, gb_in, gc_ref, ga_ref, gb_ref):
    total_comp, total_assay, _ = totals
    gc_ref[...] = gc_in[...] * (1.0 / math.sqrt(total_assay))
    ga_ref[...] = ga_in[...] * (1.0 / math.sqrt(total_comp))
    gb_ref[...] = gb_in[...] * (1.0 / math.sqrt(total_comp * total_assay))


def local(comp_emb, assay_emb, bilinear, tile_pos):
    size_cmp, size_asy = lax.axis_size("cmp"), lax.axis_size("asy")
    rows_c, width = comp_emb.shape
    rows_a = assay_emb.shape[0]
    total_comp, total_assay = rows_c * size_cmp * size_asy, rows_a * size_cmp * size_asy
    half_c, group_a = rows_c * RING, rows_a * RING
    part = width // 2 // RING
    vmem = pl.BlockSpec(memory_space=pltpu.VMEM)
    block_c, block_a = rows_c + CODE_ROWS, rows_a + CODE_ROWS
    totals = (total_comp, total_assay, width)
    shapes = [
        jax.ShapeDtypeStruct((rows_c, width), jnp.float32),
        jax.ShapeDtypeStruct((rows_a, width), jnp.float32),
        jax.ShapeDtypeStruct((width, width), jnp.float32),
    ]
    sums = (
        pl.pallas_call(
            functools.partial(kernel, totals),
            out_shape=shapes,
            in_specs=[
                pl.BlockSpec(memory_space=pltpu.SMEM),
                pl.BlockSpec(memory_space=pl.ANY),
                pl.BlockSpec(memory_space=pl.ANY),
                vmem,
            ],
            out_specs=[vmem, vmem, vmem],
            scratch_shapes=[
                pltpu.VMEM((2, half_c, width), jnp.bfloat16),
                pltpu.VMEM((RING, 2, group_a, width), jnp.bfloat16),
                pltpu.VMEM((2, half_c, width), jnp.bfloat16),
                pltpu.VMEM((RING, 2, 2 * half_c, group_a), jnp.bfloat16),
                pltpu.VMEM((2, half_c, width), jnp.float32),
                pltpu.VMEM((RING, group_a, width), jnp.float32),
                pltpu.VMEM((RING, group_a, width), jnp.float32),
                pltpu.VMEM((RING, group_a, width), jnp.float32),
                pltpu.VMEM((3, 2, block_c, width), jnp.int16),
                pltpu.VMEM((3, 2, block_c, width), jnp.int16),
                pltpu.VMEM((block_c, width), jnp.int16),
                pltpu.VMEM((block_c, width), jnp.int16),
                pltpu.VMEM((RING, 3, block_a, width), jnp.int16),
                pltpu.VMEM((RING, 3, block_a, width), jnp.int16),
                pltpu.VMEM((3, block_a, width), jnp.int16),
                pltpu.VMEM((3, block_a, width), jnp.int16),
                pltpu.VMEM((width, width), jnp.float32),
                pltpu.VMEM((3, part, width), jnp.float32),
                pltpu.VMEM((3, part // RING, width), jnp.float32),
                pltpu.VMEM((RING, part // RING, width), jnp.float32),
                pltpu.VMEM((2, part // RING, width), jnp.float32),
                pltpu.VMEM((width // 2, width), jnp.float32),
                pltpu.SemaphoreType.DMA((SENDS,)),
                pltpu.SemaphoreType.DMA((SENDS,)),
                pltpu.SemaphoreType.DMA((2,)),
            ],
            compiler_params=pltpu.CompilerParams(
                collective_id=0, has_side_effects=True, vmem_limit_bytes=58 * 2**20
            ),
            name="link_grads",
        )(tile_pos, comp_emb, assay_emb, bilinear)
    )
    return tuple(
        pl.pallas_call(
            functools.partial(scale_kernel, totals),
            out_shape=shapes,
            in_specs=[vmem, vmem, vmem],
            out_specs=[vmem, vmem, vmem],
            name="scale_grads",
        )(*sums)
    )


def solution(mesh):
    return jax.shard_map(
        local,
        mesh=mesh,
        in_specs=(P(("cmp", "asy"), None), P(("asy", "cmp"), None), P(), P("cmp", "asy")),
        out_specs=(P(("cmp", "asy"), None), P(("asy", "cmp"), None), P()),
        check_vma=False,
    )
```
